256 devices in a mesh: fsdp: 16 (over z, x_lo), ctx: 16 (over x_hi, y, core).
Axes of the slice: x: 4 (x_hi: 2, x_lo: 2; x = x_hi * 2 + x_lo), y: 4, z: 8, core: 2. Of those that a mesh axis runs over, the one named last changes fastest.
Arguments:
- q_latent: bfloat16 [16, 2048, 1536], P('fsdp', 'ctx'), may hold values from -6 to 6
- kv_compressed: bfloat16 [16, 2048, 576], P('fsdp', 'ctx'), may hold values from -6 to 6
- lengths: int32 [16], P('fsdp'), may hold values from 256 to 2048, as said below
- q_gain: float32 [1536], replicated, may hold values from 0.5 to 1.5
- kv_gain: float32 [512], replicated, may hold values from 0.5 to 1.5
- w_q_up: bfloat16 [1536, 12288], P('fsdp', 'ctx'), may hold values from -0.10844095 to 0.10844095
- w_kv_up: bfloat16 [512, 16384], P('fsdp', 'ctx'), may hold values from -0.18782524 to 0.18782524
Outputs:
- attn_out: bfloat16 [16, 2048, 8192], P('fsdp', 'ctx')
The draws below stay inside these ranges and needn't reach their ends.
Inputs may be any that keep to these rules, and one draw needn't show every extreme that they name: `lengths`: each rollout's count of valid tokens; in every draw some rollout is full (2048).
All inputs are finite; a program needn't handle non-finite values.
Results may differ from the reference program's by a relative error of at most 0.0079.
Values may be sent and summed in bfloat16 or wider, within the bound.
No kernel may reach another device: no remote copies, remote signals or barrier semaphores. Data moves between devices by JAX's collectives and lax.ppermute only.
A program may use at most 192 MiB of HBM per device.

```python
import jax
import jax.numpy as jnp
from jax import lax

HEADS = 64
QL = 1536
KVL = 512
ROPE = 64
NOPE = 128
VDIM = 128
LENGTH = 2048
ROLLOUTS = 16


def draw_lengths(key, part):
    key = jax.random.fold_in(key, 7)
    first, second = jax.random.split(key)
    values = jax.random.randint(first, (ROLLOUTS,), LENGTH // 8, LENGTH + 1)
    chosen = jax.random.randint(second, (), 0, ROLLOUTS)
    return jnp.where(jnp.arange(ROLLOUTS) == chosen, LENGTH, values).astype(jnp.int32)


def draw_q_latent(key, part):
    key = jax.random.fold_in(key, 11)
    first = jax.random.fold_in(key, 0)
    noise = jax.random.truncated_normal(first, -6.0, 6.0, (ROLLOUTS, LENGTH, QL), jnp.float32)
    return noise.astype(jnp.bfloat16)


def draw_kv_compressed(key, part):
    key = jax.random.fold_in(key, 13)
    first = jax.random.fold_in(key, 0)
    noise = jax.random.truncated_normal(first, -6.0, 6.0, (ROLLOUTS, LENGTH, KVL + ROPE), jnp.float32)
    return noise.astype(jnp.bfloat16)


def draw_w_q_up(key, part):
    key = jax.random.fold_in(key, 23)
    values = jax.random.truncated_normal(key, -4.0, 4.0, (QL, HEADS, NOPE + ROPE), jnp.float32)
    return (values * QL ** (-0.5)).reshape(QL, HEADS * (NOPE + ROPE)).astype(jnp.bfloat16)


def draw_w_kv_up(key, part):
    key = jax.random.fold_in(key, 29)
    values = jax.random.truncated_normal(key, -4.0, 4.0, (KVL, HEADS, NOPE + VDIM), jnp.float32)
    return (values * KVL ** (-0.5)).reshape(KVL, HEADS * (NOPE + VDIM)).astype(jnp.bfloat16)


def setup_inputs(seed: int = 0) -> dict:
    streams_of = jax.random.split(jax.random.key(seed), 8)
    q_latent = draw_q_latent(jax.random.fold_in(streams_of[7], 71), 0)
    kv_compressed = draw_kv_compressed(jax.random.fold_in(streams_of[7], 71), 0)
    lengths = draw_lengths(jax.random.fold_in(streams_of[7], 71), 0)
    q_gain = jnp.clip(jax.random.uniform(streams_of[3], (QL,), jnp.float32, 0.5, 1.5), 0.5, 1.5)
    kv_gain = jnp.clip(jax.random.uniform(streams_of[4], (KVL,), jnp.float32, 0.5, 1.5), 0.5, 1.5)
    w_q_up = draw_w_q_up(jax.random.fold_in(streams_of[7], 71), 0)
    w_kv_up = draw_w_kv_up(jax.random.fold_in(streams_of[7], 71), 0)
    return {"q_latent": q_latent, "kv_compressed": kv_compressed, "lengths": lengths, "q_gain": q_gain, "kv_gain": kv_gain, "w_q_up": w_q_up, "w_kv_up": w_kv_up}


def normalize(values, gain):
    wide = values.astype(jnp.float32)
    return wide * lax.rsqrt(lax.optimization_barrier(jnp.mean(wide * wide, axis=-1, keepdims=True)) + 1e-06) * gain

def angles_for(positions, half):
    inverse = 10000.0 ** (-jnp.arange(half, dtype=jnp.float32) / half)
    return positions[:, None] * inverse[None, :]

def rotate(values, angles):
    half = values.shape[-1] // 2
    first, second = (values[..., :half], values[..., half:])
    cosine, sine = (jnp.cos(angles), jnp.sin(angles))
    return jnp.concatenate([first * cosine - second * sine, second * cosine + first * sine], axis=-1)

def one_rollout(q_rows, kv_rows, length, q_gain, kv_gain, w_q_up, w_kv_up):
    positions = jnp.arange(LENGTH, dtype=jnp.float32)
    angles = angles_for(positions, ROPE // 2)
    q_norm = normalize(q_rows, q_gain).astype(jnp.bfloat16)
    kv_norm = normalize(kv_rows[:, :KVL], kv_gain).astype(jnp.bfloat16)
    key_rope = rotate(kv_rows[:, KVL:].astype(jnp.float32), angles).astype(jnp.bfloat16)
    qfull = jnp.dot(q_norm, w_q_up, preferred_element_type=jnp.float32).reshape(LENGTH, HEADS, NOPE + ROPE)
    scale = 1.0 / jnp.sqrt(jnp.float32(NOPE + ROPE))
    query = jnp.concatenate([qfull[..., :NOPE], rotate(qfull[..., NOPE:], angles[:, None, :])], axis=-1)
    query = (query * scale).astype(jnp.bfloat16)
    kvfull = jnp.dot(kv_norm, w_kv_up, preferred_element_type=jnp.float32).astype(jnp.bfloat16)
    kvfull = kvfull.reshape(LENGTH, HEADS, NOPE + VDIM)
    index = jnp.arange(LENGTH).astype(jnp.int32)
    allowed = (index[None, :] <= index[:, None]) & (index[None, :] < length)

    def one_head(packed):
        head_query, head_kv = packed
        head_key = jnp.concatenate([head_kv[:, :NOPE], key_rope], axis=-1)
        scores = jnp.dot(head_query, head_key.T, preferred_element_type=jnp.float32)
        scores = jnp.where(allowed, scores, jnp.float32(-1e+30))
        top = lax.optimization_barrier(jnp.max(scores, axis=-1, keepdims=True))
        expo = jnp.where(allowed, jnp.exp(scores - top), jnp.float32(0.0))
        probs = (expo / lax.optimization_barrier(jnp.sum(expo, axis=-1, keepdims=True))).astype(jnp.bfloat16)
        return jnp.dot(probs, head_kv[:, NOPE:], preferred_element_type=jnp.float32)
    outputs = lax.map(one_head, (jnp.transpose(query, (1, 0, 2)), jnp.transpose(kvfull, (1, 0, 2))))
    outputs = jnp.transpose(outputs, (1, 0, 2)).reshape(LENGTH, HEADS * VDIM)
    outputs = jnp.where((index < length)[:, None], outputs, jnp.float32(0.0))
    return outputs.astype(jnp.bfloat16)

def reference(q_latent, kv_compressed, lengths, q_gain, kv_gain, w_q_up, w_kv_up):

    def step(packed):
        q_rows, kv_rows, length = packed
        return one_rollout(q_rows, kv_rows, length, q_gain, kv_gain, w_q_up, w_kv_up)
    return lax.map(step, (q_latent, kv_compressed, lengths))
```

```python
import jax
import jax.numpy as jnp
from jax import lax
from jax.experimental import pallas as pl
from jax.experimental.pallas import tpu as pltpu
from jax.sharding import PartitionSpec as P

QL = 1536
KVL = 512
ROPE = 64
NOPE = 128
VDIM = 128
LOG2E = 1.4426950408889634
WIDE = QL + KVL + 128
F32 = jnp.float32
BF16 = jnp.bfloat16


def rope_tables(positions):
    half = ROPE // 2
    inverse = 10000.0 ** (-jnp.arange(half, dtype=F32) / half)
    angles = positions.astype(F32)[:, None] * inverse[None, :]
    cosine, sine = jnp.cos(angles), jnp.sin(angles)
    return (
        jnp.concatenate([cosine] * 4, axis=1),
        jnp.concatenate([-sine, -sine, sine, sine], axis=1),
    )


def normalized(values, gain):
    wide = values.astype(F32)
    return (
        wide * lax.rsqrt(jnp.mean(wide * wide, axis=-1, keepdims=True) + 1e-06) * gain
    ).astype(BF16)


def order_kernel(wq_ref, wkv_ref, w_ref):
    row = lax.broadcasted_iota(jnp.int32, (768, 768), 0)
    lane = lax.broadcasted_iota(jnp.int32, (1, 768), 1)
    rest = lane - 512
    low = rest % 128
    head = 2 * (rest // 128) + (low % 64) // 32
    source = jnp.where(
        lane < 512,
        192 * (lane // 128) + lane % 128,
        192 * head + 128 + 32 * (low // 64) + low % 32,
    )
    order = jnp.where(row == source, 1.0, 0.0).astype(BF16)
    w_ref[:, :768] = jnp.dot(wq_ref[...], order, preferred_element_type=F32).astype(BF16)
    w_ref[0:32, 768:1152] = wkv_ref[:, 0:384]
    w_ref[32:64, 768:1152] = wkv_ref[:, 384:768]
    w_ref[64:96, 768:1024] = wkv_ref[:, 768:1024]
    w_ref[64:96, 1024:1152] = jnp.zeros((32, 128), BF16)


def prepare_kernel(q_ref, kv_ref, qg_ref, kg_ref, cos_ref, sin_ref, x_ref):
    x_ref[:, :QL] = normalized(q_ref[0], qg_ref[...][None])
    x_ref[:, QL : QL + KVL] = normalized(kv_ref[0, :, :KVL], kg_ref[...][None])
    row = lax.broadcasted_iota(jnp.int32, (ROPE, 128), 0)
    lane = lax.broadcasted_iota(jnp.int32, (ROPE, 128), 1)
    spread = jnp.where(row == 32 * (lane // 64) + lane % 32, 1.0, 0.0).astype(BF16)
    key = jnp.dot(kv_ref[0, :, KVL:], spread, preferred_element_type=F32)
    rotated = key * cos_ref[...] + pltpu.roll(key, 64, 1) * sin_ref[...]
    x_ref[:, QL + KVL :] = rotated.astype(BF16)


def attend_kernel(group, nx, nw, total, *refs):
    place_ref, cos_from, sin_from = refs[:3]
    x_refs = refs[3 : 3 + nx]
    w_refs = refs[3 + nx : 3 + nx + nw]
    out_ref = refs[3 + nx + nw]
    xs, wq, wkv, qs, ks, vs, cos_ref, sin_ref, x_sem, w_sem, one_sem = refs[4 + nx + nw :]
    copies = [
        pltpu.make_async_copy(cos_from, cos_ref, one_sem.at[0]),
        pltpu.make_async_copy(sin_from, sin_ref, one_sem.at[1]),
    ]
    q_pieces = ((0, 256 * group, 256, 0), (0, 512 + 128 * group, 128, 256))
    kv_pieces = (
        ((0, 768, 384, 0), (32, 768, 128, 384)),
        ((32, 896, 256, 0), (64, 768, 256, 256)),
    )[group]
    for i in range(nw):
        first = place_ref[nx + i]
        for r in range(2):
            shard = first if r == 0 else first ^ 1
            for j, (row, column, width, to) in enumerate(q_pieces + kv_pieces):
                tall = 96 if j < 2 else 32
                at = pl.multiple_of(shard * tall, 32)
                copies.append(
                    pltpu.make_async_copy(
                        w_refs[i].at[pl.ds(96 * r + row, tall), pl.ds(column, width)],
                        (wq if j < 2 else wkv).at[pl.ds(at, tall), pl.ds(to, width)],
                        w_sem.at[i, 4 * r + j],
                    )
                )
    for i in range(nx):
        at = pl.multiple_of(place_ref[i], 128)
        copies.append(pltpu.make_async_copy(x_refs[i], xs.at[pl.ds(at, 128), :], x_sem.at[i]))
    for copy in copies:
        copy.start()
    for copy in copies:
        copy.wait()
    length = place_ref[nx + nw]
    block = 256
    lane = lax.broadcasted_iota(jnp.int32, (block, 128), 1)
    even = (lane % 64) < 32
    scale = 192.0 ** -0.5 * LOG2E
    ones = jnp.ones((block, 128), BF16)
    for b in range(total // block):
        rows = pl.ds(b * block, block)
        kv = jnp.dot(xs[rows, QL : QL + KVL], wkv[...], preferred_element_type=F32).astype(BF16)
        rope = xs[rows, QL + KVL :]
        zero = jnp.zeros_like(rope)
        for h in range(2):
            ks[h, rows, :128] = kv[:, 256 * h : 256 * h + 128]
            ks[h, rows, 128:] = jnp.where(even if h == 0 else ~even, rope, zero)
            vs[h, rows, :128] = kv[:, 256 * h + 128 : 256 * h + 256]
            vs[h, rows, 128:] = ones
        q = jnp.dot(xs[rows, :QL], wq[...], preferred_element_type=F32) * scale
        turn = q[:, 256:]
        turn = (turn * cos_ref[rows, :] + pltpu.roll(turn, 64, 1) * sin_ref[rows, :]).astype(BF16)
        for h in range(2):
            qs[h, rows, :128] = q[:, 128 * h : 128 * h + 128].astype(BF16)
            qs[h, rows, 128:] = turn
    row = lax.broadcasted_iota(jnp.int32, (block, block), 0)
    column = lax.broadcasted_iota(jnp.int32, (block, block), 1)
    for b in range(total // block):
        rows = pl.ds(b * block, block)
        for h in range(2):
            query = qs[h, rows, :]
            dims = (((1,), (1,)), ((), ()))
            last = lax.dot_general(query, ks[h, rows, :], dims, preferred_element_type=F32)
            last = jnp.where(column <= row, last, -1e30)
            top = jnp.max(last, axis=-1, keepdims=True)
            if b:
                before = lax.dot_general(
                    query, ks[h, pl.ds(0, b * block), :], dims, preferred_element_type=F32
                )
                top = jnp.maximum(top, jnp.max(before, axis=-1, keepdims=True))
            mixed = jnp.dot(
                jnp.exp2(last - top).astype(BF16), vs[h, rows, :], preferred_element_type=F32
            )
            if b:
                mixed += jnp.dot(
                    jnp.exp2(before - top).astype(BF16),
                    vs[h, pl.ds(0, b * block), :],
                    preferred_element_type=F32,
                )
            keep = lax.broadcasted_iota(jnp.int32, (block, 128), 0) + b * block < length
            result = jnp.where(keep, mixed[:, :128] / mixed[:, 128:], 0.0)
            out_ref[rows, 128 * h : 128 * h + 128] = result.astype(BF16)


def place_kernel(group, *refs):
    r_ref, out_ref, sem = refs[0], refs[-2], refs[-1]
    copies = [
        pltpu.make_async_copy(
            r_ref.at[s], out_ref.at[0, :, pl.ds(512 * s + 256 * group, 256)], sem.at[s]
        )
        for s in range(r_ref.shape[0])
    ]
    for copy in copies:
        copy.start()
    for copy in copies:
        copy.wait()


def sign(i):
    return 1 - 2 * (i % 2)


def from_ctx(x, dx, dy, dc=0):
    pairs = []
    for i in range(16):
        a, y, c = i // 8, (i // 2) % 4, i % 2
        source = ((a + dx) % 2) * 8 + ((y + dy * sign(i)) % 4) * 2 + (c + dc) % 2
        pairs.append((source, i))
    return lax.ppermute(x, "ctx", pairs)


def from_fsdp(x, dz, dx):
    pairs = []
    for f in range(16):
        for i in range(16):
            source = ((f // 2 + dz * sign(i)) % 8) * 2 + (f + dx) % 2
            pairs.append((source * 16 + i, f * 16 + i))
    return lax.ppermute(x, ("fsdp", "ctx"), pairs)


def shards(q_latent, kv_compressed, lengths, q_gain, kv_gain, w_q_up, w_kv_up):
    rows = q_latent.shape[1]
    total = rows * 16
    me = lax.axis_index("ctx")
    mine = lax.axis_index("fsdp")
    w = pl.pallas_call(
        order_kernel, out_shape=jax.ShapeDtypeStruct((96, 1152), BF16), name="order"
    )(w_q_up, w_kv_up)
    beside = from_fsdp(w, 0, 1)
    cos_own, sin_own = rope_tables(me * rows + jnp.arange(rows))
    x = pl.pallas_call(
        prepare_kernel, out_shape=jax.ShapeDtypeStruct((rows, WIDE), BF16), name="prepare"
    )(q_latent, kv_compressed, q_gain, kv_gain, cos_own, sin_own)
    barrier = lax.optimization_barrier
    x, beside = barrier((x, beside))

    across = from_ctx(x, 1, 0)
    ahead = from_ctx(x, 0, 1)
    behind = from_ctx(x, 0, -1)
    c, y, a = me % 2, (me // 2) % 4, me // 8
    plan = [(0, 0), (1, 0), (0, 1), (0, -1), (0, 2), (1, -1), (1, 1), (1, 2)]
    w_plan = [0, 1, -1, 2, -2, 3, -3, 4]
    places = []
    for core in range(2):
        d = sign(c + core)
        for dx, dy in plan:
            chip = ((a + dx) % 2) * 4 + (y + dy * d) % 4
            places.append((chip * 2 + (c + core) % 2) * rows)
    for dz in w_plan:
        places.append(((mine // 2 + dz * sign(c)) % 8) * 2 + mine % 2)
    places.append(lengths[0])
    place = jnp.stack(places).astype(jnp.int32)
    cos_all, sin_all = rope_tables(jnp.arange(total))
    pair = jnp.concatenate([w, beside], axis=0)
    ahead_w = from_fsdp(pair, 1, 0)
    behind_w = from_fsdp(pair, -1, 0)
    w_parts = [pair, ahead_w, behind_w]
    ahead_w, behind_w, across, ahead, behind, place, cos_all, sin_all = barrier(
        (ahead_w, behind_w, across, ahead, behind, place, cos_all, sin_all)
    )
    ahead_w = from_fsdp(ahead_w, 1, 0)
    behind_w = from_fsdp(behind_w, -1, 0)
    far = from_ctx(ahead, 0, 1)
    across_behind = from_ctx(across, 0, -1)
    across_ahead = from_ctx(ahead, 1, 0)
    ahead_w, behind_w, far, across_behind, across_ahead = barrier(
        (ahead_w, behind_w, far, across_behind, across_ahead)
    )
    w_parts += [ahead_w, behind_w]
    ahead_w = from_fsdp(ahead_w, 1, 0)
    behind_w = from_fsdp(behind_w, -1, 0)
    last = from_ctx(across_ahead, 0, 1)
    ahead_w, behind_w, last = barrier((ahead_w, behind_w, last))
    w_parts += [ahead_w, behind_w]
    w_parts.append(from_fsdp(ahead_w, 1, 0))

    x_parts = [x, across, ahead, behind, far, across_behind, across_ahead, last]
    x_parts += [from_ctx(part, 0, 0, 1) for part in x_parts]
    arrays = x_parts + w_parts

    anywhere = pl.BlockSpec(memory_space=pl.ANY)
    whole = pl.BlockSpec(memory_space=pltpu.VMEM)
    result = None
    for group in range(2):
        attended = pl.pallas_call(
            lambda *refs, group=group: attend_kernel(group, len(x_parts), len(w_parts), total, *refs),
            out_shape=jax.ShapeDtypeStruct((total, 256), BF16),
            in_specs=[pl.BlockSpec(memory_space=pltpu.SMEM)] + [anywhere] * (2 + len(arrays)),
            out_specs=whole,
            scratch_shapes=[
                pltpu.VMEM((total, WIDE), BF16),
                pltpu.VMEM((QL, 384), BF16),
                pltpu.VMEM((KVL, 512), BF16),
                pltpu.VMEM((2, total, 256), BF16),
                pltpu.VMEM((2, total, 256), BF16),
                pltpu.VMEM((2, total, 256), BF16),
                pltpu.VMEM((total, 128), F32),
                pltpu.VMEM((total, 128), F32),
                pltpu.SemaphoreType.DMA((len(x_parts),)),
                pltpu.SemaphoreType.DMA((len(w_parts), 8)),
                pltpu.SemaphoreType.DMA((2,)),
            ],
            compiler_params=pltpu.CompilerParams(vmem_limit_bytes=56 * 1024 * 1024),
            cost_estimate=pl.CostEstimate(
                flops=8_000_000_000, bytes_accessed=16_000_000, transcendentals=5_000_000
            ),
            name="attend",
        )(place, cos_all, sin_all, *arrays)
        returned = lax.all_to_all(
            attended.reshape(16, rows, 256), "ctx", split_axis=0, concat_axis=0, tiled=False
        )
        given = [returned] if result is None else [returned, result]
        result = pl.pallas_call(
            lambda *refs, group=group: place_kernel(group, *refs),
            out_shape=jax.ShapeDtypeStruct((1, rows, 8192), BF16),
            in_specs=[whole] + [anywhere] * (len(given) - 1),
            out_specs=anywhere,
            scratch_shapes=[pltpu.SemaphoreType.DMA((16,))],
            input_output_aliases={} if result is None else {1: 0},
            name="place",
        )(*given)
    return result


def solution(mesh):
    in_specs = (
        P("fsdp", "ctx", None),
        P("fsdp", "ctx", None),
        P("fsdp"),
        P(),
        P(),
        P("fsdp", "ctx"),
        P("fsdp", "ctx"),
    )
    out_specs = P("fsdp", "ctx", None)
    return jax.shard_map(shards, mesh=mesh, in_specs=in_specs, out_specs=out_specs, check_vma=False)
```

```python
import jax
import jax.numpy as jnp
from jax import lax
from jax.experimental import pallas as pl
from jax.experimental.pallas import tpu as pltpu
from jax.sharding import PartitionSpec as P

QL = 1536
KVL = 512
ROPE = 64
NOPE = 128
VDIM = 128
LOG2E = 1.4426950408889634
WIDE = QL + KVL + 128
F32 = jnp.float32
BF16 = jnp.bfloat16


def rope_tables(positions):
    lane = jnp.arange(128)
    inverse = 10000.0 ** (-(lane % 32).astype(F32) / 32)
    sign = jnp.where(lane < 64, -1.0, 1.0).astype(F32)
    angles = positions.astype(F32)[:, None] * inverse[None, :]
    return jnp.cos(angles), jnp.sin(angles) * sign


def normalized(values, gain):
    wide = values.astype(F32)
    return (
        wide * lax.rsqrt(jnp.mean(wide * wide, axis=-1, keepdims=True) + 1e-06) * gain
    ).astype(BF16)


def order_kernel(wq_ref, wkv_ref, w_ref):
    row = lax.broadcasted_iota(jnp.int32, (768, 768), 0)
    lane = lax.broadcasted_iota(jnp.int32, (1, 768), 1)
    rest = lane - 512
    low = rest % 128
    head = 2 * (rest // 128) + (low % 64) // 32
    source = jnp.where(
        lane < 512,
        192 * (lane // 128) + lane % 128,
        192 * head + 128 + 32 * (low // 64) + low % 32,
    )
    order = jnp.where(row == source, 1.0, 0.0).astype(BF16)
    w_ref[:, :768] = jnp.dot(wq_ref[...], order, preferred_element_type=F32).astype(BF16)
    w_ref[0:32, 768:1152] = wkv_ref[:, 0:384]
    w_ref[32:64, 768:1152] = wkv_ref[:, 384:768]
    w_ref[64:96, 768:1024] = wkv_ref[:, 768:1024]
    w_ref[64:96, 1024:1152] = jnp.zeros((32, 128), BF16)


def prepare_kernel(q_ref, kv_ref, qg_ref, kg_ref, cos_ref, sin_ref, x_ref):
    x_ref[:, :QL] = normalized(q_ref[0], qg_ref[...][None])
    x_ref[:, QL : QL + KVL] = normalized(kv_ref[0, :KVL, :].astype(F32).T, kg_ref[...][None])
    row = lax.broadcasted_iota(jnp.int32, (ROPE, 128), 0)
    lane = lax.broadcasted_iota(jnp.int32, (ROPE, 128), 1)
    spread = jnp.where(row == 32 * (lane // 64) + lane % 32, 1.0, 0.0).astype(BF16)
    key = lax.dot_general(
        kv_ref[0, KVL:, :], spread, (((0,), (0,)), ((), ())), preferred_element_type=F32
    )
    rotated = key * cos_ref[...] + pltpu.roll(key, 64, 1) * sin_ref[...]
    x_ref[:, QL + KVL :] = rotated.astype(BF16)


def project_kernel(nx, nw, *refs):
    place_ref, cos_ref, sin_ref = refs[:3]
    x_refs = refs[3 : 3 + nx]
    w_refs = refs[3 + nx : 3 + nx + nw]
    qs, ks, vs = [refs[3 + nx + nw + i : 9 + nx + nw : 3] for i in range(3)]
    wq, wkv = refs[9 + nx + nw :]
    for i in range(nw):
        first = place_ref[nx + i]
        for r in range(2):
            shard = first if r == 0 else first ^ 1
            base = 96 * r
            wq[pl.ds(pl.multiple_of(shard * 96, 32), 96), :] = w_refs[i][base : base + 96, :768]
            at = pl.ds(pl.multiple_of(shard * 32, 32), 32)
            wkv[at, 0:384] = w_refs[i][base : base + 32, 768:1152]
            wkv[at, 384:768] = w_refs[i][base + 32 : base + 64, 768:1152]
            wkv[at, 768:1024] = w_refs[i][base + 64 : base + 96, 768:1024]
    rows = x_refs[0].shape[0]
    lane = lax.broadcasted_iota(jnp.int32, (rows, 128), 1)
    even = (lane % 64) < 32
    scale = 192.0 ** -0.5 * LOG2E
    ones = jnp.ones((rows, 128), BF16)
    for j in range(nx // 2):
        pair = (x_refs[j], x_refs[nx // 2 + j])
        kv = jnp.dot(
            jnp.concatenate([ref[:, QL : QL + KVL] for ref in pair], axis=0),
            wkv[...],
            preferred_element_type=F32,
        ).astype(BF16)
        q = jnp.dot(
            jnp.concatenate([ref[:, :QL] for ref in pair], axis=0),
            wq[...],
            preferred_element_type=F32,
        )
        for part in range(2):
            at = pl.ds(pl.multiple_of(place_ref[part * (nx // 2) + j], 128), rows)
            here = slice(part * rows, (part + 1) * rows)
            rope = pair[part][:, QL + KVL :]
            zero = jnp.zeros_like(rope)
            for h in range(4):
                g, i = divmod(h, 2)
                ks[g][i, at, :128] = kv[here, 256 * h : 256 * h + 128]
                ks[g][i, at, 128:] = jnp.where(even if i == 0 else ~even, rope, zero)
                vs[g][i, at, :128] = kv[here, 256 * h + 128 : 256 * h + 256]
                vs[g][i, at, 128:] = ones
                qs[g][i, at, :128] = (q[here, 128 * h : 128 * h + 128] * scale).astype(BF16)
            for g in range(2):
                turn = q[here, 512 + 128 * g : 640 + 128 * g] * scale
                turn = turn * cos_ref[at, :] + pltpu.roll(turn, 64, 1) * sin_ref[at, :]
                for i in range(2):
                    qs[g][i, at, 128:] = turn.astype(BF16)


def attend_kernel(length_ref, *refs):
    length = length_ref[0]
    out_ref = refs[6]
    total = out_ref.shape[0]
    block = 256
    row = lax.broadcasted_iota(jnp.int32, (block, block), 0)
    column = lax.broadcasted_iota(jnp.int32, (block, block), 1)
    for b in range(total // block):
        rows = pl.ds(b * block, block)
        for h in range(4):
            qs, ks, vs = refs[3 * (h // 2) : 3 * (h // 2) + 3]
            h, lanes = h % 2, slice(128 * h, 128 * h + 128)
            query = qs[h, rows, :]
            dims = (((1,), (1,)), ((), ()))
            last = lax.dot_general(query, ks[h, rows, :], dims, preferred_element_type=F32)
            last = jnp.where(column <= row, last, -1e30)
            top = jnp.max(last, axis=-1, keepdims=True)
            if b:
                before = lax.dot_general(
                    query, ks[h, pl.ds(0, b * block), :], dims, preferred_element_type=F32
                )
                top = jnp.maximum(top, jnp.max(before, axis=-1, keepdims=True))
            mixed = jnp.dot(
                jnp.exp2(last - top).astype(BF16), vs[h, rows, :], preferred_element_type=F32
            )
            if b:
                mixed += jnp.dot(
                    jnp.exp2(before - top).astype(BF16),
                    vs[h, pl.ds(0, b * block), :],
                    preferred_element_type=F32,
                )
            keep = lax.broadcasted_iota(jnp.int32, (block, 128), 0) + b * block < length
            result = jnp.where(keep, mixed[:, :128] / mixed[:, 128:], 0.0)
            out_ref[rows, lanes] = result.astype(BF16)


IN_SMEM = pl.BlockSpec(memory_space=pltpu.SMEM)
IN_VMEM = pl.BlockSpec(memory_space=pltpu.VMEM)
MIB = 1024 * 1024
PROJECT_MIB = 12
ATTEND_MIB = 12


def project_call(place, cos_all, sin_all, x_parts, w_parts, total):
    arrays = x_parts + w_parts
    return pl.pallas_call(
        lambda *refs: project_kernel(len(x_parts), len(w_parts), *refs),
        out_shape=[jax.ShapeDtypeStruct((2, total, 256), BF16)] * 6,
        in_specs=[IN_SMEM] + [IN_VMEM] * (2 + len(arrays)),
        out_specs=[IN_VMEM] * 6,
        scratch_shapes=[pltpu.VMEM((QL, 768), BF16), pltpu.VMEM((KVL, 1024), BF16)],
        compiler_params=pltpu.CompilerParams(vmem_limit_bytes=PROJECT_MIB * MIB),
        cost_estimate=pl.CostEstimate(
            flops=7_000_000_000, bytes_accessed=26_000_000, transcendentals=0
        ),
        name="project",
    )(place, cos_all, sin_all, *arrays)


def attend_call(lengths, projected):
    total = projected[0].shape[1]
    return pl.pallas_call(
        attend_kernel,
        out_shape=jax.ShapeDtypeStruct((total, 512), BF16),
        in_specs=[IN_SMEM] + [IN_VMEM] * 6,
        out_specs=IN_VMEM,
        compiler_params=pltpu.CompilerParams(vmem_limit_bytes=ATTEND_MIB * MIB),
        cost_estimate=pl.CostEstimate(
            flops=8_000_000_000, bytes_accessed=14_000_000, transcendentals=10_000_000
        ),
        name="attend",
    )(lengths, *projected)


def place_kernel(r_ref, out_ref, sem):
    copies = [
        pltpu.make_async_copy(r_ref.at[s], out_ref.at[0, :, pl.ds(512 * s, 512)], sem.at[s])
        for s in range(r_ref.shape[0])
    ]
    for copy in copies:
        copy.start()
    for copy in copies:
        copy.wait()


def sign(i):
    return 1 - 2 * (i % 2)


def from_ctx(x, dx, dy, dc=0):
    pairs = []
    for i in range(16):
        a, y, c = i // 8, (i // 2) % 4, i % 2
        source = ((a + dx) % 2) * 8 + ((y + dy * sign(i)) % 4) * 2 + (c + dc) % 2
        pairs.append((source, i))
    return lax.ppermute(x, "ctx", pairs)


def from_fsdp(x, dz, dx):
    pairs = []
    for f in range(16):
        for i in range(16):
            source = ((f // 2 + dz * sign(i)) % 8) * 2 + (f + dx) % 2
            pairs.append((source * 16 + i, f * 16 + i))
    return lax.ppermute(x, ("fsdp", "ctx"), pairs)


def shards(q_latent, kv_compressed, lengths, q_gain, kv_gain, w_q_up, w_kv_up):
    rows = q_latent.shape[1]
    total = rows * 16
    me = lax.axis_index("ctx")
    mine = lax.axis_index("fsdp")
    w = pl.pallas_call(
        order_kernel,
        out_shape=jax.ShapeDtypeStruct((96, 1152), BF16),
        name="order",
    )(w_q_up, w_kv_up)
    beside = from_fsdp(w, 0, 1)
    cos_own, sin_own = rope_tables(me * rows + jnp.arange(rows))
    x = pl.pallas_call(
        prepare_kernel,
        out_shape=jax.ShapeDtypeStruct((rows, WIDE), BF16),
        name="prepare",
    )(q_latent, jnp.swapaxes(kv_compressed, 1, 2), q_gain, kv_gain, cos_own, sin_own)
    barrier = lax.optimization_barrier
    pair = jnp.concatenate([w, beside], axis=0)
    x, pair = barrier((x, pair))

    across = from_ctx(x, 1, 0)
    ahead = from_ctx(x, 0, 1)
    behind = from_ctx(x, 0, -1)
    c, y, a = me % 2, (me // 2) % 4, me // 8
    plan = [(0, 0), (1, 0), (0, 1), (0, -1), (0, 2), (1, -1), (1, 1), (1, 2)]
    w_plan = [0, 1, -1, 2, -2, 3, -3, 4]
    places = []
    for core in range(2):
        for dx, dy in plan:
            chip = ((a + dx) % 2) * 4 + (y + dy * sign(c)) % 4
            places.append((chip * 2 + (c + core) % 2) * rows)
    for dz in w_plan:
        places.append(((mine // 2 + dz * sign(c)) % 8) * 2 + mine % 2)
    place = jnp.stack(places).astype(jnp.int32)
    cos_all, sin_all = rope_tables(jnp.arange(total))
    ahead_w = from_fsdp(pair, 1, 0)
    behind_w = from_fsdp(pair, -1, 0)
    w_parts = [pair, ahead_w, behind_w]
    ahead_w, behind_w, across, ahead, behind, place, cos_all, sin_all = barrier(
        (ahead_w, behind_w, across, ahead, behind, place, cos_all, sin_all)
    )
    ahead_w = from_fsdp(ahead_w, 1, 0)
    behind_w = from_fsdp(behind_w, -1, 0)
    far = from_ctx(ahead, 0, 1)
    across_behind = from_ctx(across, 0, -1)
    across_ahead = from_ctx(ahead, 1, 0)
    ahead_w, behind_w, far, across_behind, across_ahead = barrier(
        (ahead_w, behind_w, far, across_behind, across_ahead)
    )
    w_parts += [ahead_w, behind_w]
    ahead_w = from_fsdp(ahead_w, 1, 0)
    behind_w = from_fsdp(behind_w, -1, 0)
    last = from_ctx(across_ahead, 0, 1)
    ahead_w, behind_w, last = barrier((ahead_w, behind_w, last))
    w_parts += [ahead_w, behind_w]
    w_parts.append(from_fsdp(ahead_w, 1, 0))

    x_parts = [x, across, ahead, behind, far, across_behind, across_ahead, last]
    x_parts += [from_ctx(x_parts[i], 0, 0, 1) for i in (0, 1, 3, 2, 4, 6, 5, 7)]

    projected = project_call(place, cos_all, sin_all, x_parts, w_parts, total)
    attended = attend_call(lengths, projected)
    returned = lax.all_to_all(
        attended.reshape(16, rows, 512), "ctx", split_axis=0, concat_axis=0, tiled=False
    )
    return pl.pallas_call(
        place_kernel,
        out_shape=jax.ShapeDtypeStruct((1, rows, 8192), BF16),
        in_specs=[IN_VMEM],
        out_specs=pl.BlockSpec(memory_space=pl.ANY),
        scratch_shapes=[pltpu.SemaphoreType.DMA((16,))],
        compiler_params=pltpu.CompilerParams(vmem_limit_bytes=4 * MIB),
        name="place",
    )(returned)


def solution(mesh):
    in_specs = (
        P("fsdp", "ctx", None),
        P("fsdp", "ctx", None),
        P("fsdp"),
        P(),
        P(),
        P("fsdp", "ctx"),
        P("fsdp", "ctx"),
    )
    out_specs = P("fsdp", "ctx", None)
    return jax.shard_map(shards, mesh=mesh, in_specs=in_specs, out_specs=out_specs, check_vma=False)
```

```python
import jax
import jax.numpy as jnp
from jax import lax
from jax.experimental import pallas as pl
from jax.experimental.pallas import tpu as pltpu
from jax.sharding import PartitionSpec as P

QL = 1536
KVL = 512
ROPE = 64
NOPE = 128
VDIM = 128
LOG2E = 1.4426950408889634
WIDE = QL + KVL + 128
F32 = jnp.float32
BF16 = jnp.bfloat16


def rope_tables(positions):
    lane = jnp.arange(128)
    inverse = 10000.0 ** (-(lane % 32).astype(F32) / 32)
    sign = jnp.where(lane < 64, -1.0, 1.0).astype(F32)
    angles = positions.astype(F32)[:, None] * inverse[None, :]
    return jnp.cos(angles), jnp.sin(angles) * sign


def normalized(values, gain):
    wide = values.astype(F32)
    return (
        wide * lax.rsqrt(jnp.mean(wide * wide, axis=-1, keepdims=True) + 1e-06) * gain
    ).astype(BF16)


def order_kernel(wq_ref, wkv_ref, w_ref):
    row = lax.broadcasted_iota(jnp.int32, (768, 768), 0)
    lane = lax.broadcasted_iota(jnp.int32, (1, 768), 1)
    rest = lane - 512
    low = rest % 128
    head = 2 * (rest // 128) + (low % 64) // 32
    source = jnp.where(
        lane < 512,
        192 * (lane // 128) + lane % 128,
        192 * head + 128 + 32 * (low // 64) + low % 32,
    )
    order = jnp.where(row == source, 1.0, 0.0).astype(BF16)
    w_ref[:, :768] = jnp.dot(wq_ref[...], order, preferred_element_type=F32).astype(BF16)
    w_ref[0:32, 768:1152] = wkv_ref[:, 0:384]
    w_ref[32:64, 768:1152] = wkv_ref[:, 384:768]
    w_ref[64:96, 768:1024] = wkv_ref[:, 768:1024]
    w_ref[64:96, 1024:1152] = jnp.zeros((32, 128), BF16)


def prepare_kernel(q_ref, kv_ref, qg_ref, kg_ref, cos_ref, sin_ref, x_ref):
    x_ref[:, :QL] = normalized(q_ref[0], qg_ref[...][None])
    x_ref[:, QL : QL + KVL] = normalized(kv_ref[0, :KVL, :].astype(F32).T, kg_ref[...][None])
    row = lax.broadcasted_iota(jnp.int32, (ROPE, 128), 0)
    lane = lax.broadcasted_iota(jnp.int32, (ROPE, 128), 1)
    spread = jnp.where(row == 32 * (lane // 64) + lane % 32, 1.0, 0.0).astype(BF16)
    key = lax.dot_general(
        kv_ref[0, KVL:, :], spread, (((0,), (0,)), ((), ())), preferred_element_type=F32
    )
    rotated = key * cos_ref[...] + pltpu.roll(key, 64, 1) * sin_ref[...]
    x_ref[:, QL + KVL :] = rotated.astype(BF16)


def assemble_kernel(nw, place_ref, *refs):
    w_refs, (wq, wkv) = refs[:nw], refs[nw:]
    for i in range(nw):
        first = place_ref[i]
        for r in range(2):
            shard = first if r == 0 else first ^ 1
            base = 96 * r
            wq[pl.ds(pl.multiple_of(shard * 96, 32), 96), :] = w_refs[i][base : base + 96, :768]
            at = pl.ds(pl.multiple_of(shard * 32, 32), 32)
            wkv[at, 0:384] = w_refs[i][base : base + 32, 768:1152]
            wkv[at, 384:768] = w_refs[i][base + 32 : base + 64, 768:1152]
            wkv[at, 768:1024] = w_refs[i][base + 64 : base + 96, 768:1024]


def project_kernel(nx, *refs):
    place_ref, cos_ref, sin_ref, wq, wkv = refs[:5]
    x_refs = refs[5 : 5 + nx]
    qs, ks, vs = [refs[5 + nx + i : 11 + nx : 3] for i in range(3)]
    rows = x_refs[0].shape[0]
    lane = lax.broadcasted_iota(jnp.int32, (rows, 128), 1)
    even = (lane % 64) < 32
    scale = 192.0 ** -0.5 * LOG2E
    ones = jnp.ones((rows, 128), BF16)
    for j in range(nx // 2):
        pair = (x_refs[j], x_refs[nx // 2 + j])
        kv = jnp.dot(
            jnp.concatenate([ref[:, QL : QL + KVL] for ref in pair], axis=0),
            wkv[...],
            preferred_element_type=F32,
        ).astype(BF16)
        q = jnp.dot(
            jnp.concatenate([ref[:, :QL] for ref in pair], axis=0),
            wq[...],
            preferred_element_type=F32,
        )
        for part in range(2):
            at = pl.ds(pl.multiple_of(place_ref[part * (nx // 2) + j], 128), rows)
            here = slice(part * rows, (part + 1) * rows)
            rope = pair[part][:, QL + KVL :]
            zero = jnp.zeros_like(rope)
            for h in range(4):
                g, i = divmod(h, 2)
                ks[g][i, at, :128] = kv[here, 256 * h : 256 * h + 128]
                ks[g][i, at, 128:] = jnp.where(even if i == 0 else ~even, rope, zero)
                vs[g][i, at, :128] = kv[here, 256 * h + 128 : 256 * h + 256]
                vs[g][i, at, 128:] = ones
                qs[g][i, at, :128] = (q[here, 128 * h : 128 * h + 128] * scale).astype(BF16)
            for g in range(2):
                turn = q[here, 512 + 128 * g : 640 + 128 * g] * scale
                turn = turn * cos_ref[at, :] + pltpu.roll(turn, 64, 1) * sin_ref[at, :]
                for i in range(2):
                    qs[g][i, at, 128:] = turn.astype(BF16)


def attend_kernel(length_ref, *refs):
    length = length_ref[0]
    out_ref = refs[6]
    total = out_ref.shape[0]
    block = 256
    row = lax.broadcasted_iota(jnp.int32, (block, block), 0)
    column = lax.broadcasted_iota(jnp.int32, (block, block), 1)
    dims = (((1,), (1,)), ((), ()))
    items = [(b, h) for b in range(total // block) for h in range(4)]

    def score(b, h):
        qs, ks = refs[3 * (h // 2)], refs[3 * (h // 2) + 1]
        rows = pl.ds(b * block, block)
        query = qs[h % 2, rows, :]
        last = lax.dot_general(query, ks[h % 2, rows, :], dims, preferred_element_type=F32)
        last = jnp.where(column <= row, last, -1e30)
        if not b:
            return None, last
        keys = ks[h % 2, pl.ds(0, b * block), :]
        return lax.dot_general(query, keys, dims, preferred_element_type=F32), last

    def mix(b, h, before, last):
        vs = refs[3 * (h // 2) + 2]
        rows = pl.ds(b * block, block)
        top = jnp.max(last, axis=-1, keepdims=True)
        if b:
            top = jnp.maximum(top, jnp.max(before, axis=-1, keepdims=True))
        mixed = jnp.dot(
            jnp.exp2(last - top).astype(BF16), vs[h % 2, rows, :], preferred_element_type=F32
        )
        if b:
            mixed += jnp.dot(
                jnp.exp2(before - top).astype(BF16),
                vs[h % 2, pl.ds(0, b * block), :],
                preferred_element_type=F32,
            )
        keep = lax.broadcasted_iota(jnp.int32, (block, 128), 0) + b * block < length
        result = jnp.where(keep, mixed[:, :128] / mixed[:, 128:], 0.0)
        out_ref[rows, 128 * h : 128 * h + 128] = result.astype(BF16)

    ready = [score(*item) for item in items[:1]]
    for i, item in enumerate(items):
        if i + 1 < len(items):
            ready.append(score(*items[i + 1]))
        mix(*item, *ready.pop(0))


IN_SMEM = pl.BlockSpec(memory_space=pltpu.SMEM)
IN_VMEM = pl.BlockSpec(memory_space=pltpu.VMEM)
MIB = 1024 * 1024
PROJECT_MIB = 12
ATTEND_MIB = 12
ASSEMBLE_BYTES = 30_000_000


def assemble_call(place, w_parts):
    return pl.pallas_call(
        lambda *refs: assemble_kernel(len(w_parts), *refs),
        out_shape=[
            jax.ShapeDtypeStruct((QL, 768), BF16),
            jax.ShapeDtypeStruct((KVL, 1024), BF16),
        ],
        in_specs=[IN_SMEM] + [IN_VMEM] * len(w_parts),
        out_specs=[IN_VMEM] * 2,
        compiler_params=pltpu.CompilerParams(vmem_limit_bytes=4 * MIB),
        cost_estimate=pl.CostEstimate(flops=0, bytes_accessed=ASSEMBLE_BYTES, transcendentals=0),
        name="assemble",
    )(place, *w_parts)


def project_call(place, cos_all, sin_all, x_parts, weights, total):
    return pl.pallas_call(
        lambda *refs: project_kernel(len(x_parts), *refs),
        out_shape=[jax.ShapeDtypeStruct((2, total, 256), BF16)] * 6,
        in_specs=[IN_SMEM] + [IN_VMEM] * (4 + len(x_parts)),
        out_specs=[IN_VMEM] * 6,
        compiler_params=pltpu.CompilerParams(vmem_limit_bytes=PROJECT_MIB * MIB),
        cost_estimate=pl.CostEstimate(
            flops=7_000_000_000, bytes_accessed=26_000_000, transcendentals=0
        ),
        name="project",
    )(place, cos_all, sin_all, *weights, *x_parts)


def attend_call(lengths, projected):
    total = projected[0].shape[1]
    return pl.pallas_call(
        attend_kernel,
        out_shape=jax.ShapeDtypeStruct((total, 512), BF16),
        in_specs=[IN_SMEM] + [IN_VMEM] * 6,
        out_specs=IN_VMEM,
        compiler_params=pltpu.CompilerParams(vmem_limit_bytes=ATTEND_MIB * MIB),
        cost_estimate=pl.CostEstimate(
            flops=8_000_000_000, bytes_accessed=14_000_000, transcendentals=10_000_000
        ),
        name="attend",
    )(lengths, *projected)


def place_kernel(r_ref, out_ref, sem):
    copies = [
        pltpu.make_async_copy(r_ref.at[s], out_ref.at[0, :, pl.ds(512 * s, 512)], sem.at[s])
        for s in range(r_ref.shape[0])
    ]
    for copy in copies:
        copy.start()
    for copy in copies:
        copy.wait()


def sign(i):
    return 1 - 2 * (i % 2)


def from_ctx(x, dx, dy, dc=0):
    pairs = []
    for i in range(16):
        a, y, c = i // 8, (i // 2) % 4, i % 2
        source = ((a + dx) % 2) * 8 + ((y + dy * sign(i)) % 4) * 2 + (c + dc) % 2
        pairs.append((source, i))
    return lax.ppermute(x, "ctx", pairs)


def from_fsdp(x, dz, dx):
    pairs = []
    for f in range(16):
        for i in range(16):
            source = ((f // 2 + dz * sign(i)) % 8) * 2 + (f + dx) % 2
            pairs.append((source * 16 + i, f * 16 + i))
    return lax.ppermute(x, ("fsdp", "ctx"), pairs)


def shards(q_latent, kv_compressed, lengths, q_gain, kv_gain, w_q_up, w_kv_up):
    rows = q_latent.shape[1]
    total = rows * 16
    me = lax.axis_index("ctx")
    mine = lax.axis_index("fsdp")
    w = pl.pallas_call(
        order_kernel,
        out_shape=jax.ShapeDtypeStruct((96, 1152), BF16),
        name="order",
    )(w_q_up, w_kv_up)
    beside = from_fsdp(w, 0, 1)
    cos_own, sin_own = rope_tables(me * rows + jnp.arange(rows))
    x = pl.pallas_call(
        prepare_kernel,
        out_shape=jax.ShapeDtypeStruct((rows, WIDE), BF16),
        name="prepare",
    )(q_latent, jnp.swapaxes(kv_compressed, 1, 2), q_gain, kv_gain, cos_own, sin_own)
    barrier = lax.optimization_barrier
    x, beside = barrier((x, beside))

    across = from_ctx(x, 1, 0)
    ahead = from_ctx(x, 0, 1)
    behind = from_ctx(x, 0, -1)
    c, y, a = me % 2, (me // 2) % 4, me // 8
    plan = [(0, 0), (1, 0), (0, 1), (0, -1), (0, 2), (1, -1), (1, 1), (1, 2)]
    w_plan = [0, 1, -1, 2, -2, 3, -3, 4]
    places = []
    for core in range(2):
        for dx, dy in plan:
            chip = ((a + dx) % 2) * 4 + (y + dy * sign(c)) % 4
            places.append((chip * 2 + (c + core) % 2) * rows)
    w_places = []
    for dz in w_plan:
        w_places.append(((mine // 2 + dz * sign(c)) % 8) * 2 + mine % 2)
    place = jnp.stack(places).astype(jnp.int32)
    w_place = jnp.stack(w_places).astype(jnp.int32)
    cos_all, sin_all = rope_tables(jnp.arange(total))
    pair = jnp.concatenate([w, beside], axis=0)
    ahead_w = from_fsdp(pair, 1, 0)
    behind_w = from_fsdp(pair, -1, 0)
    w_parts = [pair, ahead_w, behind_w]
    ahead_w, behind_w, across, ahead, behind, place, w_place, cos_all, sin_all = barrier(
        (ahead_w, behind_w, across, ahead, behind, place, w_place, cos_all, sin_all)
    )
    ahead_w = from_fsdp(ahead_w, 1, 0)
    behind_w = from_fsdp(behind_w, -1, 0)
    far = from_ctx(ahead, 0, 1)
    across_behind = from_ctx(across, 0, -1)
    across_ahead = from_ctx(ahead, 1, 0)
    ahead_w, behind_w, far, across_behind, across_ahead = barrier(
        (ahead_w, behind_w, far, across_behind, across_ahead)
    )
    w_parts += [ahead_w, behind_w]
    ahead_w = from_fsdp(ahead_w, 1, 0)
    behind_w = from_fsdp(behind_w, -1, 0)
    last = from_ctx(across_ahead, 0, 1)
    ahead_w, behind_w, last = barrier((ahead_w, behind_w, last))
    w_parts += [ahead_w, behind_w]
    w_parts.append(from_fsdp(ahead_w, 1, 0))

    x_parts = [x, across, ahead, behind, far, across_behind, across_ahead, last]
    x_parts += [from_ctx(x_parts[i], 0, 0, 1) for i in (0, 1, 3, 2, 4, 6, 5, 7)]

    weights = assemble_call(w_place, w_parts)
    projected = project_call(place, cos_all, sin_all, x_parts, weights, total)
    attended = attend_call(lengths, projected)
    returned = lax.all_to_all(
        attended.reshape(16, rows, 512), "ctx", split_axis=0, concat_axis=0, tiled=False
    )
    return pl.pallas_call(
        place_kernel,
        out_shape=jax.ShapeDtypeStruct((1, rows, 8192), BF16),
        in_specs=[IN_VMEM],
        out_specs=pl.BlockSpec(memory_space=pl.ANY),
        scratch_shapes=[pltpu.SemaphoreType.DMA((16,))],
        compiler_params=pltpu.CompilerParams(vmem_limit_bytes=4 * MIB),
        name="place",
    )(returned)


def solution(mesh):
    in_specs = (
        P("fsdp", "ctx", None),
        P("fsdp", "ctx", None),
        P("fsdp"),
        P(),
        P(),
        P("fsdp", "ctx"),
        P("fsdp", "ctx"),
    )
    out_specs = P("fsdp", "ctx", None)
    return jax.shard_map(shards, mesh=mesh, in_specs=in_specs, out_specs=out_specs, check_vma=False)
```

```python
import jax
import jax.numpy as jnp
from jax import lax
from jax.experimental import pallas as pl
from jax.experimental.pallas import tpu as pltpu
from jax.sharding import PartitionSpec as P

QL = 1536
KVL = 512
ROPE = 64
NOPE = 128
VDIM = 128
LOG2E = 1.4426950408889634
WIDE = QL + KVL + 128
F32 = jnp.float32
BF16 = jnp.bfloat16


def rope_tables(positions):
    lane = jnp.arange(128)
    inverse = 10000.0 ** (-(lane % 32).astype(F32) / 32)
    sign = jnp.where(lane < 64, -1.0, 1.0).astype(F32)
    angles = positions.astype(F32)[:, None] * inverse[None, :]
    return jnp.cos(angles), jnp.sin(angles) * sign


def normalized(values, gain):
    wide = values.astype(F32)
    return (
        wide * lax.rsqrt(jnp.mean(wide * wide, axis=-1, keepdims=True) + 1e-06) * gain
    ).astype(BF16)


def order_kernel(wq_ref, wkv_ref, w_ref):
    row = lax.broadcasted_iota(jnp.int32, (768, 768), 0)
    lane = lax.broadcasted_iota(jnp.int32, (1, 768), 1)
    rest = lane - 512
    low = rest % 128
    head = 2 * (rest // 128) + (low % 64) // 32
    source = jnp.where(
        lane < 512,
        192 * (lane // 128) + lane % 128,
        192 * head + 128 + 32 * (low // 64) + low % 32,
    )
    order = jnp.where(row == source, 1.0, 0.0).astype(BF16)
    w_ref[:, :768] = jnp.dot(wq_ref[...], order, preferred_element_type=F32).astype(BF16)
    w_ref[0:32, 768:1152] = wkv_ref[:, 0:384]
    w_ref[32:64, 768:1152] = wkv_ref[:, 384:768]
    w_ref[64:96, 768:1024] = wkv_ref[:, 768:1024]
    w_ref[64:96, 1024:1152] = jnp.zeros((32, 128), BF16)


def prepare_kernel(q_ref, kv_ref, qg_ref, kg_ref, cos_ref, sin_ref, x_ref):
    x_ref[:, :QL] = normalized(q_ref[0], qg_ref[...][None])
    x_ref[:, QL : QL + KVL] = normalized(kv_ref[0, :KVL, :].astype(F32).T, kg_ref[...][None])
    row = lax.broadcasted_iota(jnp.int32, (ROPE, 128), 0)
    lane = lax.broadcasted_iota(jnp.int32, (ROPE, 128), 1)
    spread = jnp.where(row == 32 * (lane // 64) + lane % 32, 1.0, 0.0).astype(BF16)
    key = lax.dot_general(
        kv_ref[0, KVL:, :], spread, (((0,), (0,)), ((), ())), preferred_element_type=F32
    )
    rotated = key * cos_ref[...] + pltpu.roll(key, 64, 1) * sin_ref[...]
    x_ref[:, QL + KVL :] = rotated.astype(BF16)


def assemble_kernel(nw, place_ref, *refs):
    w_refs, (wq, wkv) = refs[:nw], refs[nw:]
    for i in range(nw):
        first = place_ref[i]
        for r in range(2):
            shard = first if r == 0 else first ^ 1
            base = 96 * r
            wq[pl.ds(pl.multiple_of(shard * 96, 32), 96), :] = w_refs[i][base : base + 96, :768]
            at = pl.ds(pl.multiple_of(shard * 32, 32), 32)
            wkv[at, 0:384] = w_refs[i][base : base + 32, 768:1152]
            wkv[at, 384:768] = w_refs[i][base + 32 : base + 64, 768:1152]
            wkv[at, 768:1024] = w_refs[i][base + 64 : base + 96, 768:1024]


def project_kernel(nx, *refs):
    place_ref, cos_ref, sin_ref, wq, wkv = refs[:5]
    x_refs = refs[5 : 5 + nx]
    qs, ks, vs = [refs[5 + nx + i : 11 + nx : 3] for i in range(3)]
    rows = x_refs[0].shape[0]
    lane = lax.broadcasted_iota(jnp.int32, (rows, 128), 1)
    even = (lane % 64) < 32
    scale = 192.0 ** -0.5 * LOG2E
    ones = jnp.ones((rows, 128), BF16)
    for j in range(nx // 2):
        pair = (x_refs[j], x_refs[nx // 2 + j])
        kv = jnp.dot(
            jnp.concatenate([ref[:, QL : QL + KVL] for ref in pair], axis=0),
            wkv[...],
            preferred_element_type=F32,
        ).astype(BF16)
        q = jnp.dot(
            jnp.concatenate([ref[:, :QL] for ref in pair], axis=0),
            wq[...],
            preferred_element_type=F32,
        )
        for part in range(2):
            at = pl.ds(pl.multiple_of(place_ref[part * (nx // 2) + j], 128), rows)
            here = slice(part * rows, (part + 1) * rows)
            rope = pair[part][:, QL + KVL :]
            zero = jnp.zeros_like(rope)
            for h in range(4):
                g, i = divmod(h, 2)
                ks[g][i, at, :128] = kv[here, 256 * h : 256 * h + 128]
                ks[g][i, at, 128:] = jnp.where(even if i == 0 else ~even, rope, zero)
                vs[g][i, at, :128] = kv[here, 256 * h + 128 : 256 * h + 256]
                vs[g][i, at, 128:] = ones
                qs[g][i, at, :128] = (q[here, 128 * h : 128 * h + 128] * scale).astype(BF16)
            for g in range(2):
                turn = q[here, 512 + 128 * g : 640 + 128 * g] * scale
                turn = turn * cos_ref[at, :] + pltpu.roll(turn, 64, 1) * sin_ref[at, :]
                for i in range(2):
                    qs[g][i, at, 128:] = turn.astype(BF16)


def attend_kernel(length_ref, *refs):
    length = length_ref[0]
    out_ref = refs[6]
    total = out_ref.shape[0]
    block = 256
    row = lax.broadcasted_iota(jnp.int32, (block, block), 0)
    column = lax.broadcasted_iota(jnp.int32, (block, block), 1)
    dims = (((1,), (1,)), ((), ()))
    items = [(b, h) for b in range(total // block) for h in range(4)]

    def score(b, h):
        qs, ks = refs[3 * (h // 2)], refs[3 * (h // 2) + 1]
        rows = pl.ds(b * block, block)
        query = qs[h % 2, rows, :]
        last = lax.dot_general(query, ks[h % 2, rows, :], dims, preferred_element_type=F32)
        last = jnp.where(column <= row, last, -1e30)
        if not b:
            return None, last
        keys = ks[h % 2, pl.ds(0, b * block), :]
        return lax.dot_general(query, keys, dims, preferred_element_type=F32), last

    def mix(b, h, before, last):
        vs = refs[3 * (h // 2) + 2]
        rows = pl.ds(b * block, block)
        top = jnp.max(last, axis=-1, keepdims=True)
        if b:
            top = jnp.maximum(top, jnp.max(before, axis=-1, keepdims=True))
        mixed = jnp.dot(
            jnp.exp2(last - top).astype(BF16), vs[h % 2, rows, :], preferred_element_type=F32
        )
        if b:
            mixed += jnp.dot(
                jnp.exp2(before - top).astype(BF16),
                vs[h % 2, pl.ds(0, b * block), :],
                preferred_element_type=F32,
            )
        keep = lax.broadcasted_iota(jnp.int32, (block, 128), 0) + b * block < length
        result = jnp.where(keep, mixed[:, :128] / mixed[:, 128:], 0.0)
        out_ref[rows, 128 * h : 128 * h + 128] = result.astype(BF16)

    ready = [score(*item) for item in items[:1]]
    for i, item in enumerate(items):
        if i + 1 < len(items):
            ready.append(score(*items[i + 1]))
        mix(*item, *ready.pop(0))


IN_SMEM = pl.BlockSpec(memory_space=pltpu.SMEM)
IN_VMEM = pl.BlockSpec(memory_space=pltpu.VMEM)
MIB = 1024 * 1024
PROJECT_MIB = 20
ATTEND_MIB = 12
ASSEMBLE_BYTES = 30_000_000


def assemble_call(place, w_parts):
    return pl.pallas_call(
        lambda *refs: assemble_kernel(len(w_parts), *refs),
        out_shape=[
            jax.ShapeDtypeStruct((QL, 768), BF16),
            jax.ShapeDtypeStruct((KVL, 1024), BF16),
        ],
        in_specs=[IN_SMEM] + [IN_VMEM] * len(w_parts),
        out_specs=[IN_VMEM] * 2,
        compiler_params=pltpu.CompilerParams(vmem_limit_bytes=4 * MIB),
        cost_estimate=pl.CostEstimate(flops=0, bytes_accessed=ASSEMBLE_BYTES, transcendentals=0),
        name="assemble",
    )(place, *w_parts)


def project_call(place, cos_all, sin_all, x_parts, weights, total):
    return pl.pallas_call(
        lambda *refs: project_kernel(len(x_parts), *refs),
        out_shape=[jax.ShapeDtypeStruct((2, total, 256), BF16)] * 6,
        in_specs=[IN_SMEM] + [IN_VMEM] * (4 + len(x_parts)),
        out_specs=[IN_VMEM] * 6,
        compiler_params=pltpu.CompilerParams(vmem_limit_bytes=PROJECT_MIB * MIB),
        cost_estimate=pl.CostEstimate(
            flops=7_000_000_000, bytes_accessed=26_000_000, transcendentals=0
        ),
        name="project",
    )(place, cos_all, sin_all, *weights, *x_parts)


def attend_call(lengths, projected):
    total = projected[0].shape[1]
    return pl.pallas_call(
        attend_kernel,
        out_shape=jax.ShapeDtypeStruct((total, 512), BF16),
        in_specs=[IN_SMEM] + [IN_VMEM] * 6,
        out_specs=IN_VMEM,
        compiler_params=pltpu.CompilerParams(vmem_limit_bytes=ATTEND_MIB * MIB),
        cost_estimate=pl.CostEstimate(
            flops=8_000_000_000, bytes_accessed=14_000_000, transcendentals=10_000_000
        ),
        name="attend",
    )(lengths, *projected)


def place_kernel(r_ref, out_ref, sem):
    copies = [
        pltpu.make_async_copy(r_ref.at[s], out_ref.at[0, :, pl.ds(512 * s, 512)], sem.at[s])
        for s in range(r_ref.shape[0])
    ]
    for copy in copies:
        copy.start()
    for copy in copies:
        copy.wait()


def sign(i):
    return 1 - 2 * (i % 2)


def from_ctx(x, dx, dy, dc=0):
    pairs = []
    for i in range(16):
        a, y, c = i // 8, (i // 2) % 4, i % 2
        source = ((a + dx) % 2) * 8 + ((y + dy * sign(i)) % 4) * 2 + (c + dc) % 2
        pairs.append((source, i))
    return lax.ppermute(x, "ctx", pairs)


def from_fsdp(x, dz, dx):
    pairs = []
    for f in range(16):
        for i in range(16):
            source = ((f // 2 + dz * sign(i)) % 8) * 2 + (f + dx) % 2
            pairs.append((source * 16 + i, f * 16 + i))
    return lax.ppermute(x, ("fsdp", "ctx"), pairs)


def shards(q_latent, kv_compressed, lengths, q_gain, kv_gain, w_q_up, w_kv_up):
    rows = q_latent.shape[1]
    total = rows * 16
    me = lax.axis_index("ctx")
    mine = lax.axis_index("fsdp")
    w = pl.pallas_call(
        order_kernel,
        out_shape=jax.ShapeDtypeStruct((96, 1152), BF16),
        name="order",
    )(w_q_up, w_kv_up)
    beside = from_fsdp(w, 0, 1)
    cos_own, sin_own = rope_tables(me * rows + jnp.arange(rows))
    x = pl.pallas_call(
        prepare_kernel,
        out_shape=jax.ShapeDtypeStruct((rows, WIDE), BF16),
        name="prepare",
    )(q_latent, jnp.swapaxes(kv_compressed, 1, 2), q_gain, kv_gain, cos_own, sin_own)
    barrier = lax.optimization_barrier
    x, beside = barrier((x, beside))

    across = from_ctx(x, 1, 0)
    ahead = from_ctx(x, 0, 1)
    behind = from_ctx(x, 0, -1)
    c, y, a = me % 2, (me // 2) % 4, me // 8
    plan = [(0, 0), (1, 0), (0, 1), (0, -1), (0, 2), (1, -1), (1, 1), (1, 2)]
    w_plan = [0, 1, -1, 2, -2, 3, -3, 4]
    places = []
    for core in range(2):
        for dx, dy in plan:
            chip = ((a + dx) % 2) * 4 + (y + dy * sign(c)) % 4
            places.append((chip * 2 + (c + core) % 2) * rows)
    w_places = []
    for dz in w_plan:
        w_places.append(((mine // 2 + dz * sign(c)) % 8) * 2 + mine % 2)
    place = jnp.stack(places).astype(jnp.int32)
    w_place = jnp.stack(w_places).astype(jnp.int32)
    cos_all, sin_all = rope_tables(jnp.arange(total))
    pair = jnp.concatenate([w, beside], axis=0)
    ahead_w = from_fsdp(pair, 1, 0)
    behind_w = from_fsdp(pair, -1, 0)
    w_parts = [pair, ahead_w, behind_w]
    ahead_w, behind_w, across, ahead, behind, place, w_place, cos_all, sin_all = barrier(
        (ahead_w, behind_w, across, ahead, behind, place, w_place, cos_all, sin_all)
    )
    ahead_w = from_fsdp(ahead_w, 1, 0)
    behind_w = from_fsdp(behind_w, -1, 0)
    far = from_ctx(ahead, 0, 1)
    across_behind = from_ctx(across, 0, -1)
    across_ahead = from_ctx(ahead, 1, 0)
    ahead_w, behind_w, far, across_behind, across_ahead = barrier(
        (ahead_w, behind_w, far, across_behind, across_ahead)
    )
    w_parts += [ahead_w, behind_w]
    ahead_w = from_fsdp(ahead_w, 1, 0)
    behind_w = from_fsdp(behind_w, -1, 0)
    last = from_ctx(across_ahead, 0, 1)
    ahead_w, behind_w, last = barrier((ahead_w, behind_w, last))
    w_parts += [ahead_w, behind_w]
    w_parts.append(from_fsdp(ahead_w, 1, 0))

    x_parts = [x, across, ahead, behind, far, across_behind, across_ahead, last]
    x_parts += [from_ctx(x_parts[i], 0, 0, 1) for i in (0, 1, 3, 2, 4, 6, 5, 7)]

    weights = assemble_call(w_place, w_parts)
    projected = project_call(place, cos_all, sin_all, x_parts, weights, total)
    attended = attend_call(lengths, projected)
    returned = lax.all_to_all(
        attended.reshape(16, rows, 512), "ctx", split_axis=0, concat_axis=0, tiled=False
    )
    return pl.pallas_call(
        place_kernel,
        out_shape=jax.ShapeDtypeStruct((1, rows, 8192), BF16),
        in_specs=[IN_VMEM],
        out_specs=pl.BlockSpec(memory_space=pl.ANY),
        scratch_shapes=[pltpu.SemaphoreType.DMA((16,))],
        compiler_params=pltpu.CompilerParams(vmem_limit_bytes=4 * MIB),
        name="place",
    )(returned)


def solution(mesh):
    in_specs = (
        P("fsdp", "ctx", None),
        P("fsdp", "ctx", None),
        P("fsdp"),
        P(),
        P(),
        P("fsdp", "ctx"),
        P("fsdp", "ctx"),
    )
    out_specs = P("fsdp", "ctx", None)
    return jax.shard_map(shards, mesh=mesh, in_specs=in_specs, out_specs=out_specs, check_vma=False)
```

```python
import jax
import jax.numpy as jnp
from jax import lax
from jax.experimental import pallas as pl
from jax.experimental.pallas import tpu as pltpu
from jax.sharding import PartitionSpec as P

QL = 1536
KVL = 512
ROPE = 64
NOPE = 128
VDIM = 128
LOG2E = 1.4426950408889634
WIDE = QL + KVL + 128
F32 = jnp.float32
BF16 = jnp.bfloat16


def rope_tables(positions):
    lane = jnp.arange(128)
    inverse = 10000.0 ** (-(lane % 32).astype(F32) / 32)
    sign = jnp.where(lane < 64, -1.0, 1.0).astype(F32)
    angles = positions.astype(F32)[:, None] * inverse[None, :]
    return jnp.cos(angles), jnp.sin(angles) * sign


def normalized(values, gain):
    wide = values.astype(F32)
    return (
        wide * lax.rsqrt(jnp.mean(wide * wide, axis=-1, keepdims=True) + 1e-06) * gain
    ).astype(BF16)


def order_kernel(wq_ref, wkv_ref, w_ref):
    row = lax.broadcasted_iota(jnp.int32, (768, 768), 0)
    lane = lax.broadcasted_iota(jnp.int32, (1, 768), 1)
    rest = lane - 512
    low = rest % 128
    head = 2 * (rest // 128) + (low % 64) // 32
    source = jnp.where(
        lane < 512,
        192 * (lane // 128) + lane % 128,
        192 * head + 128 + 32 * (low // 64) + low % 32,
    )
    order = jnp.where(row == source, 1.0, 0.0).astype(BF16)
    w_ref[:, :768] = jnp.dot(wq_ref[...], order, preferred_element_type=F32).astype(BF16)
    w_ref[0:32, 768:1152] = wkv_ref[:, 0:384]
    w_ref[32:64, 768:1152] = wkv_ref[:, 384:768]
    w_ref[64:96, 768:1024] = wkv_ref[:, 768:1024]
    w_ref[64:96, 1024:1152] = jnp.zeros((32, 128), BF16)


def prepare_kernel(q_ref, kv_ref, qg_ref, kg_ref, cos_ref, sin_ref, x_ref):
    x_ref[:, :QL] = normalized(q_ref[0], qg_ref[...][None])
    x_ref[:, QL : QL + KVL] = normalized(kv_ref[0, :KVL, :].astype(F32).T, kg_ref[...][None])
    row = lax.broadcasted_iota(jnp.int32, (ROPE, 128), 0)
    lane = lax.broadcasted_iota(jnp.int32, (ROPE, 128), 1)
    spread = jnp.where(row == 32 * (lane // 64) + lane % 32, 1.0, 0.0).astype(BF16)
    key = lax.dot_general(
        kv_ref[0, KVL:, :], spread, (((0,), (0,)), ((), ())), preferred_element_type=F32
    )
    rotated = key * cos_ref[...] + pltpu.roll(key, 64, 1) * sin_ref[...]
    x_ref[:, QL + KVL :] = rotated.astype(BF16)


def assemble_kernel(nw, place_ref, *refs):
    w_refs, (wq, wkv) = refs[:nw], refs[nw:]
    for i in range(nw):
        first = place_ref[i]
        for r in range(2):
            shard = first if r == 0 else first ^ 1
            base = 96 * r
            wq[pl.ds(pl.multiple_of(shard * 96, 32), 96), :] = w_refs[i][base : base + 96, :768]
            at = pl.ds(pl.multiple_of(shard * 32, 32), 32)
            wkv[at, 0:384] = w_refs[i][base : base + 32, 768:1152]
            wkv[at, 384:768] = w_refs[i][base + 32 : base + 64, 768:1152]
            wkv[at, 768:1024] = w_refs[i][base + 64 : base + 96, 768:1024]


def project_kernel(nx, *refs):
    place_ref, cos_ref, sin_ref, wq, wkv = refs[:5]
    x_refs = refs[5 : 5 + nx]
    qs, ks, vs = [refs[5 + nx + i : 11 + nx : 3] for i in range(3)]
    rows = x_refs[0].shape[0]
    lane = lax.broadcasted_iota(jnp.int32, (rows, 128), 1)
    even = (lane % 64) < 32
    scale = 192.0 ** -0.5 * LOG2E
    ones = jnp.ones((rows, 128), BF16)
    for j in range(nx // 2):
        pair = (x_refs[j], x_refs[nx // 2 + j])
        kv = jnp.dot(
            jnp.concatenate([ref[:, QL : QL + KVL] for ref in pair], axis=0),
            wkv[...],
            preferred_element_type=F32,
        ).astype(BF16)
        q = jnp.dot(
            jnp.concatenate([ref[:, :QL] for ref in pair], axis=0),
            wq[...],
            preferred_element_type=F32,
        )
        for part in range(2):
            at = pl.ds(pl.multiple_of(place_ref[part * (nx // 2) + j], 128), rows)
            here = slice(part * rows, (part + 1) * rows)
            rope = pair[part][:, QL + KVL :]
            zero = jnp.zeros_like(rope)
            for h in range(4):
                g, i = divmod(h, 2)
                ks[g][i, at, :128] = kv[here, 256 * h : 256 * h + 128]
                ks[g][i, at, 128:] = jnp.where(even if i == 0 else ~even, rope, zero)
                vs[g][i, at, :128] = kv[here, 256 * h + 128 : 256 * h + 256]
                vs[g][i, at, 128:] = ones
                qs[g][i, at, :128] = (q[here, 128 * h : 128 * h + 128] * scale).astype(BF16)
            for g in range(2):
                turn = q[here, 512 + 128 * g : 640 + 128 * g] * scale
                turn = turn * cos_ref[at, :] + pltpu.roll(turn, 64, 1) * sin_ref[at, :]
                for i in range(2):
                    qs[g][i, at, 128:] = turn.astype(BF16)


def attend_kernel(length_ref, *refs):
    length = length_ref[0]
    out_ref = refs[6]
    total = out_ref.shape[0]
    block = 256
    row = lax.broadcasted_iota(jnp.int32, (block, block), 0)
    column = lax.broadcasted_iota(jnp.int32, (block, block), 1)
    dims = (((1,), (1,)), ((), ()))
    items = [(b, h) for b in range(total // block) for h in range(4)]

    def score(b, h):
        qs, ks = refs[3 * (h // 2)], refs[3 * (h // 2) + 1]
        rows = pl.ds(b * block, block)
        query = qs[h % 2, rows, :]
        last = lax.dot_general(query, ks[h % 2, rows, :], dims, preferred_element_type=F32)
        last = jnp.where(column <= row, last, -1e30)
        if not b:
            return None, last
        keys = ks[h % 2, pl.ds(0, b * block), :]
        return lax.dot_general(query, keys, dims, preferred_element_type=F32), last

    def mix(b, h, before, last):
        vs = refs[3 * (h // 2) + 2]
        rows = pl.ds(b * block, block)
        top = jnp.max(last, axis=-1, keepdims=True)
        if b:
            top = jnp.maximum(top, jnp.max(before, axis=-1, keepdims=True))
        mixed = jnp.dot(
            jnp.exp2(last - top).astype(BF16), vs[h % 2, rows, :], preferred_element_type=F32
        )
        if b:
            mixed += jnp.dot(
                jnp.exp2(before - top).astype(BF16),
                vs[h % 2, pl.ds(0, b * block), :],
                preferred_element_type=F32,
            )
        keep = lax.broadcasted_iota(jnp.int32, (block, 128), 0) + b * block < length
        result = jnp.where(keep, mixed[:, :128] / mixed[:, 128:], 0.0)
        out_ref[rows, 128 * h : 128 * h + 128] = result.astype(BF16)

    ready = [score(*item) for item in items[:1]]
    for i, item in enumerate(items):
        if i + 1 < len(items):
            ready.append(score(*items[i + 1]))
        mix(*item, *ready.pop(0))


IN_SMEM = pl.BlockSpec(memory_space=pltpu.SMEM)
IN_VMEM = pl.BlockSpec(memory_space=pltpu.VMEM)
MIB = 1024 * 1024
PROJECT_MIB = 20
ATTEND_MIB = 12
ASSEMBLE_BYTES = 30_000_000


def assemble_call(place, w_parts):
    return pl.pallas_call(
        lambda *refs: assemble_kernel(len(w_parts), *refs),
        out_shape=[
            jax.ShapeDtypeStruct((QL, 768), BF16),
            jax.ShapeDtypeStruct((KVL, 1024), BF16),
        ],
        in_specs=[IN_SMEM] + [IN_VMEM] * len(w_parts),
        out_specs=[IN_VMEM] * 2,
        compiler_params=pltpu.CompilerParams(vmem_limit_bytes=4 * MIB),
        cost_estimate=pl.CostEstimate(flops=0, bytes_accessed=ASSEMBLE_BYTES, transcendentals=0),
        name="assemble",
    )(place, *w_parts)


def project_call(place, cos_all, sin_all, x_parts, weights, total):
    return pl.pallas_call(
        lambda *refs: project_kernel(len(x_parts), *refs),
        out_shape=[jax.ShapeDtypeStruct((2, total, 256), BF16)] * 6,
        in_specs=[IN_SMEM] + [IN_VMEM] * (4 + len(x_parts)),
        out_specs=[IN_VMEM] * 6,
        compiler_params=pltpu.CompilerParams(vmem_limit_bytes=PROJECT_MIB * MIB),
        cost_estimate=pl.CostEstimate(
            flops=7_000_000_000, bytes_accessed=26_000_000, transcendentals=0
        ),
        name="project",
    )(place, cos_all, sin_all, *weights, *x_parts)


def attend_call(lengths, projected):
    total = projected[0].shape[1]
    return pl.pallas_call(
        attend_kernel,
        out_shape=jax.ShapeDtypeStruct((total, 512), BF16),
        in_specs=[IN_SMEM] + [IN_VMEM] * 6,
        out_specs=IN_VMEM,
        compiler_params=pltpu.CompilerParams(vmem_limit_bytes=ATTEND_MIB * MIB),
        cost_estimate=pl.CostEstimate(
            flops=8_000_000_000, bytes_accessed=14_000_000, transcendentals=10_000_000
        ),
        name="attend",
    )(lengths, *projected)


def place_kernel(r_ref, out_ref, sem):
    copies = [
        pltpu.make_async_copy(r_ref.at[s], out_ref.at[0, :, pl.ds(512 * s, 512)], sem.at[s])
        for s in range(r_ref.shape[0])
    ]
    for copy in copies:
        copy.start()
    for copy in copies:
        copy.wait()


def sign(i):
    return 1 - 2 * (i % 2)


def from_ctx(x, dx, dy, dc=0):
    pairs = []
    for i in range(16):
        a, y, c = i // 8, (i // 2) % 4, i % 2
        source = ((a + dx) % 2) * 8 + ((y + dy * sign(i)) % 4) * 2 + (c + dc) % 2
        pairs.append((source, i))
    return lax.ppermute(x, "ctx", pairs)


def from_fsdp(x, dz, dx):
    pairs = []
    for f in range(16):
        for i in range(16):
            source = ((f // 2 + dz * sign(i)) % 8) * 2 + (f + dx) % 2
            pairs.append((source * 16 + i, f * 16 + i))
    return lax.ppermute(x, ("fsdp", "ctx"), pairs)


def shards(q_latent, kv_compressed, lengths, q_gain, kv_gain, w_q_up, w_kv_up):
    rows = q_latent.shape[1]
    total = rows * 16
    me = lax.axis_index("ctx")
    mine = lax.axis_index("fsdp")
    w = pl.pallas_call(
        order_kernel,
        out_shape=jax.ShapeDtypeStruct((96, 1152), BF16),
        name="order",
    )(w_q_up, w_kv_up)
    beside = from_fsdp(w, 0, 1)
    cos_own, sin_own = rope_tables(me * rows + jnp.arange(rows))
    x = pl.pallas_call(
        prepare_kernel,
        out_shape=jax.ShapeDtypeStruct((rows, WIDE), BF16),
        name="prepare",
    )(q_latent, jnp.swapaxes(kv_compressed, 1, 2), q_gain, kv_gain, cos_own, sin_own)
    barrier = lax.optimization_barrier
    behind, ahead = from_ctx(x, 0, -1), from_ctx(x, 0, 1)
    x, beside = barrier((x, beside))

    across = from_ctx(x, 1, 0)
    c, y, a = me % 2, (me // 2) % 4, me // 8
    plan = [(0, 0), (1, 0), (0, 1), (0, -1), (0, 2), (1, -1), (1, 1), (1, 2)]
    w_plan = [0, 1, -1, 2, -2, 3, -3, 4]
    places = []
    for core in range(2):
        for dx, dy in plan:
            chip = ((a + dx) % 2) * 4 + (y + dy * sign(c)) % 4
            places.append((chip * 2 + (c + core) % 2) * rows)
    w_places = []
    for dz in w_plan:
        w_places.append(((mine // 2 + dz * sign(c)) % 8) * 2 + mine % 2)
    place = jnp.stack(places).astype(jnp.int32)
    w_place = jnp.stack(w_places).astype(jnp.int32)
    cos_all, sin_all = rope_tables(jnp.arange(total))
    pair = jnp.concatenate([w, beside], axis=0)
    ahead_w = from_fsdp(pair, 1, 0)
    behind_w = from_fsdp(pair, -1, 0)
    w_parts = [pair, ahead_w, behind_w]
    ahead_w, behind_w, across, ahead, behind, place, w_place, cos_all, sin_all = barrier(
        (ahead_w, behind_w, across, ahead, behind, place, w_place, cos_all, sin_all)
    )
    ahead_w = from_fsdp(ahead_w, 1, 0)
    behind_w = from_fsdp(behind_w, -1, 0)
    far = from_ctx(ahead, 0, 1)
    across_behind = from_ctx(across, 0, -1)
    across_ahead = from_ctx(ahead, 1, 0)
    ahead_w, behind_w, far, across_behind, across_ahead = barrier(
        (ahead_w, behind_w, far, across_behind, across_ahead)
    )
    w_parts += [ahead_w, behind_w]
    ahead_w = from_fsdp(ahead_w, 1, 0)
    behind_w = from_fsdp(behind_w, -1, 0)
    last = from_ctx(across_ahead, 0, 1)
    ahead_w, behind_w, last = barrier((ahead_w, behind_w, last))
    w_parts += [ahead_w, behind_w]
    w_parts.append(from_fsdp(ahead_w, 1, 0))

    x_parts = [x, across, ahead, behind, far, across_behind, across_ahead, last]
    x_parts += [from_ctx(x_parts[i], 0, 0, 1) for i in (0, 1, 3, 2, 4, 6, 5, 7)]

    weights = assemble_call(w_place, w_parts)
    projected = project_call(place, cos_all, sin_all, x_parts, weights, total)
    attended = attend_call(lengths, projected)
    returned = lax.all_to_all(
        attended.reshape(16, rows, 512), "ctx", split_axis=0, concat_axis=0, tiled=False
    )
    return pl.pallas_call(
        place_kernel,
        out_shape=jax.ShapeDtypeStruct((1, rows, 8192), BF16),
        in_specs=[IN_VMEM],
        out_specs=pl.BlockSpec(memory_space=pl.ANY),
        scratch_shapes=[pltpu.SemaphoreType.DMA((16,))],
        compiler_params=pltpu.CompilerParams(vmem_limit_bytes=4 * MIB),
        name="place",
    )(returned)


def solution(mesh):
    in_specs = (
        P("fsdp", "ctx", None),
        P("fsdp", "ctx", None),
        P("fsdp"),
        P(),
        P(),
        P("fsdp", "ctx"),
        P("fsdp", "ctx"),
    )
    out_specs = P("fsdp", "ctx", None)
    return jax.shard_map(shards, mesh=mesh, in_specs=in_specs, out_specs=out_specs, check_vma=False)
```

```python
import jax
import jax.numpy as jnp
from jax import lax
from jax.experimental import pallas as pl
from jax.experimental.pallas import tpu as pltpu
from jax.sharding import PartitionSpec as P

QL = 1536
KVL = 512
ROPE = 64
NOPE = 128
VDIM = 128
LOG2E = 1.4426950408889634
WIDE = QL + KVL + 128
F32 = jnp.float32
BF16 = jnp.bfloat16


def rope_tables(positions):
    lane = jnp.arange(128)
    inverse = 10000.0 ** (-(lane % 32).astype(F32) / 32)
    sign = jnp.where(lane < 64, -1.0, 1.0).astype(F32)
    angles = positions.astype(F32)[:, None] * inverse[None, :]
    return jnp.cos(angles), jnp.sin(angles) * sign


def normalized(values, gain):
    wide = values.astype(F32)
    return (
        wide * lax.rsqrt(jnp.mean(wide * wide, axis=-1, keepdims=True) + 1e-06) * gain
    ).astype(BF16)


def order_kernel(wq_ref, wkv_ref, w_ref):
    row = lax.broadcasted_iota(jnp.int32, (768, 768), 0)
    lane = lax.broadcasted_iota(jnp.int32, (1, 768), 1)
    rest = lane - 512
    low = rest % 128
    head = 2 * (rest // 128) + (low % 64) // 32
    source = jnp.where(
        lane < 512,
        192 * (lane // 128) + lane % 128,
        192 * head + 128 + 32 * (low // 64) + low % 32,
    )
    order = jnp.where(row == source, 1.0, 0.0).astype(BF16)
    w_ref[:, :768] = jnp.dot(wq_ref[...], order, preferred_element_type=F32).astype(BF16)
    w_ref[0:32, 768:1152] = wkv_ref[:, 0:384]
    w_ref[32:64, 768:1152] = wkv_ref[:, 384:768]
    w_ref[64:96, 768:1024] = wkv_ref[:, 768:1024]
    w_ref[64:96, 1024:1152] = jnp.zeros((32, 128), BF16)


def prepare_kernel(q_ref, kv_ref, qg_ref, kg_ref, cos_ref, sin_ref, x_ref):
    x_ref[:, :QL] = normalized(q_ref[0], qg_ref[...][None])
    x_ref[:, QL : QL + KVL] = normalized(kv_ref[0, :KVL, :].astype(F32).T, kg_ref[...][None])
    row = lax.broadcasted_iota(jnp.int32, (ROPE, 128), 0)
    lane = lax.broadcasted_iota(jnp.int32, (ROPE, 128), 1)
    spread = jnp.where(row == 32 * (lane // 64) + lane % 32, 1.0, 0.0).astype(BF16)
    key = lax.dot_general(
        kv_ref[0, KVL:, :], spread, (((0,), (0,)), ((), ())), preferred_element_type=F32
    )
    rotated = key * cos_ref[...] + pltpu.roll(key, 64, 1) * sin_ref[...]
    x_ref[:, QL + KVL :] = rotated.astype(BF16)


def assemble_kernel(nw, place_ref, *refs):
    w_refs, (wq, wkv) = refs[:nw], refs[nw:]
    for i in range(nw):
        first = place_ref[i]
        for r in range(2):
            shard = first if r == 0 else first ^ 1
            base = 96 * r
            wq[pl.ds(pl.multiple_of(shard * 96, 32), 96), :] = w_refs[i][base : base + 96, :768]
            at = pl.ds(pl.multiple_of(shard * 32, 32), 32)
            wkv[at, 0:384] = w_refs[i][base : base + 32, 768:1152]
            wkv[at, 384:768] = w_refs[i][base + 32 : base + 64, 768:1152]
            wkv[at, 768:1024] = w_refs[i][base + 64 : base + 96, 768:1024]


def project_kernel(nx, *refs):
    place_ref, cos_ref, sin_ref, wq, wkv = refs[:5]
    x_refs = refs[5 : 5 + nx]
    qs, ks, vs = [refs[5 + nx + i : 11 + nx : 3] for i in range(3)]
    rows = x_refs[0].shape[0]
    lane = lax.broadcasted_iota(jnp.int32, (rows, 128), 1)
    even = (lane % 64) < 32
    scale = 192.0 ** -0.5 * LOG2E
    ones = jnp.ones((rows, 128), BF16)
    for j in range(nx // 2):
        pair = (x_refs[j], x_refs[nx // 2 + j])
        kv = jnp.dot(
            jnp.concatenate([ref[:, QL : QL + KVL] for ref in pair], axis=0),
            wkv[...],
            preferred_element_type=F32,
        ).astype(BF16)
        q = jnp.dot(
            jnp.concatenate([ref[:, :QL] for ref in pair], axis=0),
            wq[...],
            preferred_element_type=F32,
        )
        for part in range(2):
            at = pl.ds(pl.multiple_of(place_ref[part * (nx // 2) + j], 128), rows)
            here = slice(part * rows, (part + 1) * rows)
            rope = pair[part][:, QL + KVL :]
            zero = jnp.zeros_like(rope)
            for h in range(4):
                g, i = divmod(h, 2)
                ks[g][i, at, :128] = kv[here, 256 * h : 256 * h + 128]
                ks[g][i, at, 128:] = jnp.where(even if i == 0 else ~even, rope, zero)
                vs[g][i, at, :128] = kv[here, 256 * h + 128 : 256 * h + 256]
                vs[g][i, at, 128:] = ones
                qs[g][i, at, :128] = (q[here, 128 * h : 128 * h + 128] * scale).astype(BF16)
            for g in range(2):
                turn = q[here, 512 + 128 * g : 640 + 128 * g] * scale
                turn = turn * cos_ref[at, :] + pltpu.roll(turn, 64, 1) * sin_ref[at, :]
                for i in range(2):
                    qs[g][i, at, 128:] = turn.astype(BF16)


def attend_kernel(length_ref, *refs):
    length = length_ref[0]
    out_ref = refs[6]
    total = out_ref.shape[0]
    block = 256
    row = lax.broadcasted_iota(jnp.int32, (block, block), 0)
    column = lax.broadcasted_iota(jnp.int32, (block, block), 1)
    dims = (((1,), (1,)), ((), ()))
    items = [(b, h) for b in range(total // block) for h in range(4)]

    def score(b, h):
        qs, ks = refs[3 * (h // 2)], refs[3 * (h // 2) + 1]
        rows = pl.ds(b * block, block)
        query = qs[h % 2, rows, :]
        last = lax.dot_general(query, ks[h % 2, rows, :], dims, preferred_element_type=F32)
        last = jnp.where(column <= row, last, -1e30)
        if not b:
            return None, last
        keys = ks[h % 2, pl.ds(0, b * block), :]
        return lax.dot_general(query, keys, dims, preferred_element_type=F32), last

    def mix(b, h, before, last):
        vs = refs[3 * (h // 2) + 2]
        rows = pl.ds(b * block, block)
        top = jnp.max(last, axis=-1, keepdims=True)
        if b:
            top = jnp.maximum(top, jnp.max(before, axis=-1, keepdims=True))
        mixed = jnp.dot(
            jnp.exp2(last - top).astype(BF16), vs[h % 2, rows, :], preferred_element_type=F32
        )
        if b:
            mixed += jnp.dot(
                jnp.exp2(before - top).astype(BF16),
                vs[h % 2, pl.ds(0, b * block), :],
                preferred_element_type=F32,
            )
        keep = lax.broadcasted_iota(jnp.int32, (block, 128), 0) + b * block < length
        result = jnp.where(keep, mixed[:, :128] / mixed[:, 128:], 0.0)
        out_ref[rows, 128 * h : 128 * h + 128] = result.astype(BF16)

    ready = [score(*item) for item in items[:1]]
    for i, item in enumerate(items):
        if i + 1 < len(items):
            ready.append(score(*items[i + 1]))
        mix(*item, *ready.pop(0))


IN_SMEM = pl.BlockSpec(memory_space=pltpu.SMEM)
IN_VMEM = pl.BlockSpec(memory_space=pltpu.VMEM)
MIB = 1024 * 1024
PROJECT_MIB = 20
ATTEND_MIB = 12
ASSEMBLE_BYTES = 30_000_000


def assemble_call(place, w_parts):
    return pl.pallas_call(
        lambda *refs: assemble_kernel(len(w_parts), *refs),
        out_shape=[
            jax.ShapeDtypeStruct((QL, 768), BF16),
            jax.ShapeDtypeStruct((KVL, 1024), BF16),
        ],
        in_specs=[IN_SMEM] + [IN_VMEM] * len(w_parts),
        out_specs=[IN_VMEM] * 2,
        compiler_params=pltpu.CompilerParams(vmem_limit_bytes=4 * MIB),
        cost_estimate=pl.CostEstimate(flops=0, bytes_accessed=ASSEMBLE_BYTES, transcendentals=0),
        name="assemble",
    )(place, *w_parts)


def project_call(place, cos_all, sin_all, x_parts, weights, total):
    return pl.pallas_call(
        lambda *refs: project_kernel(len(x_parts), *refs),
        out_shape=[jax.ShapeDtypeStruct((2, total, 256), BF16)] * 6,
        in_specs=[IN_SMEM] + [IN_VMEM] * (4 + len(x_parts)),
        out_specs=[IN_VMEM] * 6,
        compiler_params=pltpu.CompilerParams(vmem_limit_bytes=PROJECT_MIB * MIB),
        cost_estimate=pl.CostEstimate(
            flops=7_000_000_000, bytes_accessed=26_000_000, transcendentals=0
        ),
        name="project",
    )(place, cos_all, sin_all, *weights, *x_parts)


def attend_call(lengths, projected):
    total = projected[0].shape[1]
    return pl.pallas_call(
        attend_kernel,
        out_shape=jax.ShapeDtypeStruct((total, 512), BF16),
        in_specs=[IN_SMEM] + [IN_VMEM] * 6,
        out_specs=IN_VMEM,
        compiler_params=pltpu.CompilerParams(vmem_limit_bytes=ATTEND_MIB * MIB),
        cost_estimate=pl.CostEstimate(
            flops=8_000_000_000, bytes_accessed=14_000_000, transcendentals=10_000_000
        ),
        name="attend",
    )(lengths, *projected)


def place_kernel(r_ref, out_ref, sem):
    copies = [
        pltpu.make_async_copy(r_ref.at[s], out_ref.at[0, :, pl.ds(512 * s, 512)], sem.at[s])
        for s in range(r_ref.shape[0])
    ]
    for copy in copies:
        copy.start()
    for copy in copies:
        copy.wait()


def sign(i):
    return 1 - 2 * (i % 2)


def from_ctx(x, dx, dy, dc=0):
    pairs = []
    for i in range(16):
        a, y, c = i // 8, (i // 2) % 4, i % 2
        source = ((a + dx) % 2) * 8 + ((y + dy * sign(i)) % 4) * 2 + (c + dc) % 2
        pairs.append((source, i))
    return lax.ppermute(x, "ctx", pairs)


def from_fsdp(x, dz, dx):
    pairs = []
    for f in range(16):
        for i in range(16):
            source = ((f // 2 + dz * sign(i)) % 8) * 2 + (f + dx) % 2
            pairs.append((source * 16 + i, f * 16 + i))
    return lax.ppermute(x, ("fsdp", "ctx"), pairs)


def shards(q_latent, kv_compressed, lengths, q_gain, kv_gain, w_q_up, w_kv_up):
    rows = q_latent.shape[1]
    total = rows * 16
    me = lax.axis_index("ctx")
    mine = lax.axis_index("fsdp")
    w = pl.pallas_call(
        order_kernel,
        out_shape=jax.ShapeDtypeStruct((96, 1152), BF16),
        name="order",
    )(w_q_up, w_kv_up)
    beside = from_fsdp(w, 0, 1)
    cos_own, sin_own = rope_tables(me * rows + jnp.arange(rows))
    x = pl.pallas_call(
        prepare_kernel,
        out_shape=jax.ShapeDtypeStruct((rows, WIDE), BF16),
        name="prepare",
    )(q_latent, jnp.swapaxes(kv_compressed, 1, 2), q_gain, kv_gain, cos_own, sin_own)
    barrier = lax.optimization_barrier
    behind, ahead = from_ctx(x, 0, -1), from_ctx(x, 0, 1)
    x, beside = barrier((x, beside))

    across = from_ctx(x, 1, 0)
    c, y, a = me % 2, (me // 2) % 4, me // 8
    plan = [(0, 0), (1, 0), (0, 1), (0, -1), (0, 2), (1, -1), (1, 1), (1, 2)]
    w_plan = [0, 1, -1, 2, -2, 3, -3, 4]
    places = []
    for core in range(2):
        for dx, dy in plan:
            chip = ((a + dx) % 2) * 4 + (y + dy * sign(c)) % 4
            places.append((chip * 2 + (c + core) % 2) * rows)
    w_places = []
    for dz in w_plan:
        w_places.append(((mine // 2 + dz * sign(c)) % 8) * 2 + mine % 2)
    place = jnp.stack(places).astype(jnp.int32)
    w_place = jnp.stack(w_places).astype(jnp.int32)
    cos_all, sin_all = rope_tables(jnp.arange(total))
    pair = jnp.concatenate([w, beside], axis=0)
    ahead_w = from_fsdp(pair, 1, 0)
    behind_w = from_fsdp(pair, -1, 0)
    w_parts = [pair, ahead_w, behind_w]
    ahead_w, behind_w, across, ahead, behind, place, w_place, cos_all, sin_all = barrier(
        (ahead_w, behind_w, across, ahead, behind, place, w_place, cos_all, sin_all)
    )
    ahead_w = from_fsdp(ahead_w, 1, 0)
    behind_w = from_fsdp(behind_w, -1, 0)
    far = from_ctx(ahead, 0, 1)
    across_behind = from_ctx(across, 0, -1)
    across_ahead = from_ctx(ahead, 1, 0)
    ahead_w, behind_w, far, across_behind, across_ahead = barrier(
        (ahead_w, behind_w, far, across_behind, across_ahead)
    )
    w_parts += [ahead_w, behind_w]
    ahead_w = from_fsdp(ahead_w, 1, 0)
    behind_w = from_fsdp(behind_w, -1, 0)
    last = from_ctx(across_ahead, 0, 1)
    w_parts += [ahead_w, behind_w]
    w_parts.append(from_fsdp(ahead_w, 1, 0))

    x_parts = [x, across, ahead, behind, far, across_behind, across_ahead, last]
    x_parts += [from_ctx(x_parts[i], 0, 0, 1) for i in (0, 1, 3, 2, 4, 6, 5, 7)]

    weights = assemble_call(w_place, w_parts)
    projected = project_call(place, cos_all, sin_all, x_parts, weights, total)
    attended = attend_call(lengths, projected)
    returned = lax.all_to_all(
        attended.reshape(16, rows, 512), "ctx", split_axis=0, concat_axis=0, tiled=False
    )
    return pl.pallas_call(
        place_kernel,
        out_shape=jax.ShapeDtypeStruct((1, rows, 8192), BF16),
        in_specs=[IN_VMEM],
        out_specs=pl.BlockSpec(memory_space=pl.ANY),
        scratch_shapes=[pltpu.SemaphoreType.DMA((16,))],
        compiler_params=pltpu.CompilerParams(vmem_limit_bytes=4 * MIB),
        name="place",
    )(returned)


def solution(mesh):
    in_specs = (
        P("fsdp", "ctx", None),
        P("fsdp", "ctx", None),
        P("fsdp"),
        P(),
        P(),
        P("fsdp", "ctx"),
        P("fsdp", "ctx"),
    )
    out_specs = P("fsdp", "ctx", None)
    return jax.shard_map(shards, mesh=mesh, in_specs=in_specs, out_specs=out_specs, check_vma=False)
```
